512 devices in a mesh: dp: 16 (over z_hi, x, core), blk: 32 (over y, z_lo).
Axes of the slice: x: 4, y: 4, z: 16 (z_hi: 2, z_lo: 8; z = z_hi * 8 + z_lo), core: 2. Of those that a mesh axis runs over, the one named last changes fastest.
Arguments:
- policy_context: bfloat16 [16384, 4096], P('dp', 'blk'), may hold values from -6 to 6
- frozen_context: bfloat16 [16384, 4096], P('dp', 'blk'), may hold values from -6 to 6
- policy_stream: bfloat16 [4608, 16384], P('blk', 'dp'), may hold values from -6 to 6
- frozen_stream: bfloat16 [4608, 16384], P('blk', 'dp'), may hold values from -6 to 6
- targets: bfloat16 [4608, 16384], P('blk', 'dp'), may hold values from -0.09375 to 0.09375
- policy_gain: float32 [4608], P('blk'), may hold values from 0.1 to 1.9
- frozen_gain: float32 [4608], P('blk'), may hold values from 0.1 to 1.9
- policy_weight: bfloat16 [4608, 4096], P('blk'), may hold values from -0.09375 to 0.09375
- frozen_weight: bfloat16 [4608, 4096], P('blk'), may hold values from -0.09375 to 0.09375
- valid_lengths: int32 [256], P('dp'), may hold values from 16 to 64, as said below
- pair_rows: int32 [128, 2], replicated, may hold values from 0 to 255, as said below
Outputs:
- weight_grad: float32 [4608, 4096], P('blk', 'dp')
- margins: float32 [128], replicated
- loss: float32 [], replicated
The draws below stay inside these ranges and needn't reach their ends.
Inputs may be any that keep to these rules, and one draw needn't show every extreme that they name: `valid_lengths`: at least one sequence has length 64. `pair_rows`: every sequence appears in exactly one pair, as chosen or as rejected.
All inputs are finite; a program needn't handle non-finite values.
Results may differ from the reference program's by a relative error of at most 0.0029.
Values may be sent and summed in bfloat16 or wider, within the bound.
No kernel may reach another device: no remote copies, remote signals or barrier semaphores. Data moves between devices by JAX's collectives and lax.ppermute only.
A program may use at most 64 MiB of HBM per device.

```python
import jax
import jax.numpy as jnp
from jax import lax

D = 4608
HD = 4096
LEN = 64
TOKENS = 16384
SEQS = 256
PAIRS = 128


def draw_valid_lengths(key, part):
    key = jax.random.fold_in(key, 11)
    first, second = jax.random.split(key)
    drawn = jax.random.randint(first, (SEQS,), LEN // 4, LEN + 1)
    picked = jax.random.randint(second, (), 0, SEQS)
    places = jnp.arange(SEQS, dtype=jnp.int32)
    return jnp.where(places == picked, LEN, drawn).astype(jnp.int32)


def draw_pair_rows(key, part):
    key = jax.random.fold_in(key, 23)
    order = jax.random.permutation(key, SEQS)
    return order.reshape(PAIRS, 2).astype(jnp.int32)


def level_of(own_key, extent, pieces, low, top_value):
    level, own = 1.0, jax.random.fold_in(own_key, 6)
    for dim, shards_of in pieces:
        steps = jnp.exp(jax.random.uniform(jax.random.fold_in(own, dim), (shards_of,), jnp.float32, low / len(pieces), top_value / len(pieces)))
        level = level * jnp.repeat(steps, extent[dim] // shards_of).reshape([-1 if axis == dim else 1 for axis in range(len(extent))])
    return level


def centred(key, extent, spread, most, shards=(), held_as=jnp.bfloat16):
    result = spread * jax.random.normal(key, extent, jnp.float32)
    if shards:
        result = result * level_of(key, extent, shards, -0.22, 0.18)
    return jnp.clip(result, -most, most).astype(held_as)


def setup_inputs(seed: int = 0) -> dict:
    arg_keys = jax.random.split(jax.random.key(seed), 12)
    policy_context = centred(arg_keys[0], (TOKENS, HD), 1.0, 6.0, ((0, 16), (1, 32)))
    frozen_context = centred(arg_keys[1], (TOKENS, HD), 1.0, 6.0, ((0, 16), (1, 32)))
    policy_stream = centred(arg_keys[2], (D, TOKENS), 1.0, 6.0, ((0, 32), (1, 16)))
    frozen_stream = centred(arg_keys[3], (D, TOKENS), 1.0, 6.0, ((0, 32), (1, 16)))
    targets = centred(arg_keys[4], (D, TOKENS), D ** -0.5, 0.09375, ((0, 32), (1, 16)))
    policy_gain = jnp.clip(1.0 + 0.18 * jax.random.normal(arg_keys[5], (D,), jnp.float32), 0.1, 1.9)
    frozen_gain = jnp.clip(1.0 + 0.18 * jax.random.normal(arg_keys[6], (D,), jnp.float32), 0.1, 1.9)
    policy_weight = centred(arg_keys[7], (D, HD), HD ** -0.5, 0.09375, ((0, 32),))
    frozen_weight = centred(arg_keys[8], (D, HD), HD ** -0.5, 0.09375, ((0, 32),))
    valid_lengths = draw_valid_lengths(jax.random.fold_in(arg_keys[11], 71), 0)
    pair_rows = draw_pair_rows(jax.random.fold_in(arg_keys[11], 71), 0)
    return dict(policy_context=policy_context, frozen_context=frozen_context, policy_stream=policy_stream, frozen_stream=frozen_stream, targets=targets, policy_gain=policy_gain, frozen_gain=frozen_gain, policy_weight=policy_weight, frozen_weight=frozen_weight, valid_lengths=valid_lengths, pair_rows=pair_rows)


beta_scale = 0.1
epsilon = 1e-06

def model_scores(context, weight, stream, gain, targets, valid):
    product = lax.dot_general(weight, context, (((1,), (1,)), ((), ())), preferred_element_type=jnp.float32)
    hidden = stream.astype(jnp.float32) + product
    square = lax.optimization_barrier(jnp.sum(hidden * hidden, axis=0))
    scale = lax.rsqrt(square / D + epsilon)
    weighted = gain[:, None] * targets.astype(jnp.float32)
    dotted = lax.optimization_barrier(jnp.sum(hidden * weighted, axis=0))
    score = scale * dotted
    sums = lax.optimization_barrier(jnp.sum(score.reshape(SEQS, LEN) * valid, axis=1))
    return (hidden, scale, weighted, dotted, sums)

def reference(policy_context, frozen_context, policy_stream, frozen_stream, targets, policy_gain, frozen_gain, policy_weight, frozen_weight, valid_lengths, pair_rows):
    positions = lax.broadcasted_iota(jnp.int32, (SEQS, LEN), 1)
    valid = (positions < valid_lengths[:, None]).astype(jnp.float32)
    policy_hidden, policy_scale, policy_weighted, policy_dotted, policy_sums = model_scores(policy_context, policy_weight, policy_stream, policy_gain, targets, valid)
    frozen_sums = model_scores(frozen_context, frozen_weight, frozen_stream, frozen_gain, targets, valid)[4]
    gaps = policy_sums - frozen_sums
    margins = beta_scale * (gaps[pair_rows[:, 0]] - gaps[pair_rows[:, 1]])
    loss = jnp.sum(jax.nn.softplus(-margins))
    slopes = -jax.nn.sigmoid(-margins)
    coef = jnp.zeros((SEQS,), jnp.float32)
    coef = coef.at[pair_rows[:, 0]].add(beta_scale * slopes)
    coef = coef.at[pair_rows[:, 1]].add(-beta_scale * slopes)
    token_coef = (coef[:, None] * valid).reshape(SEQS * LEN)
    step_size = token_coef * policy_scale
    correction = policy_dotted * policy_scale * policy_scale / D
    hidden_grad = (step_size[None, :] * (policy_weighted - policy_hidden * correction[None, :])).astype(jnp.bfloat16)
    weight_grad = jnp.dot(hidden_grad, policy_context, preferred_element_type=jnp.float32)
    return (weight_grad, margins, loss)
```

```python
import jax
import jax.numpy as jnp
from jax import lax
from jax.sharding import Mesh, PartitionSpec as P

D = 4608
NY = 4
NX = 4

beta_scale = 0.1
epsilon = 1e-06


def spread(value, axes, count):
    return lax.all_to_all(jnp.broadcast_to(value[None], (count,) + value.shape), axes, 0, 0)


def swap(count, bit):
    return [(i, i ^ bit) for i in range(count)]


def contract_part(weight):
    rows, features = weight.shape
    parts = weight.reshape(rows, NY, features // NY).transpose(1, 0, 2)
    return lax.all_to_all(parts, "y", 0, 0)


def hidden_of(weight_part, context_part, stream):
    slots, rows, features = weight_part.shape
    partial = lax.dot_general(
        weight_part.reshape(slots * rows, features),
        context_part,
        (((1,), (1,)), ((), ())),
        preferred_element_type=jnp.float32,
    ).astype(jnp.bfloat16)
    parts = lax.all_to_all(partial.reshape(slots, rows, -1), "y", 0, 0)
    return stream.astype(jnp.float32) + jnp.sum(parts.astype(jnp.float32), axis=0)


def shards(
    policy_context,
    frozen_context,
    policy_stream,
    frozen_stream,
    targets,
    policy_gain,
    frozen_gain,
    policy_weight,
    frozen_weight,
    valid_lengths,
    pair_rows,
):
    rows, tokens_here = policy_stream.shape
    seqs_here = valid_lengths.shape[0]
    seq_len = tokens_here // seqs_here
    z_hi, x, core = lax.axis_index("zh"), lax.axis_index("x"), lax.axis_index("c")

    both = lax.all_gather(
        jnp.concatenate([policy_context, frozen_context], 0), "zl", axis=1, tiled=True
    )
    policy_columns, frozen_columns = both[:tokens_here], both[tokens_here:]
    frozen_part = contract_part(frozen_weight)
    policy_part = contract_part(policy_weight)
    all_targets = spread(targets, "y", NY)
    all_gain = spread(policy_gain, "y", NY)

    frozen_hidden = hidden_of(frozen_part, frozen_columns, frozen_stream)
    policy_hidden = hidden_of(policy_part, policy_columns, policy_stream)
    target_values = targets.astype(jnp.float32)
    policy_weighted = policy_gain[:, None] * target_values
    frozen_weighted = frozen_gain[:, None] * target_values
    stats = jnp.stack(
        [
            jnp.sum(policy_hidden * policy_hidden, axis=0),
            jnp.sum(policy_hidden * policy_weighted, axis=0),
            jnp.sum(frozen_hidden * frozen_hidden, axis=0),
            jnp.sum(frozen_hidden * frozen_weighted, axis=0),
        ]
    )
    stats = jnp.sum(spread(stats, "y", NY), axis=0)
    stats = jnp.sum(spread(stats, "zl", 8), axis=0)
    all_hidden = spread(policy_hidden.astype(jnp.bfloat16), "y", NY)

    policy_scale = lax.rsqrt(stats[0] / D + epsilon)
    frozen_scale = lax.rsqrt(stats[2] / D + epsilon)
    policy_dotted = stats[1]
    gap_of_token = policy_scale * policy_dotted - frozen_scale * stats[3]
    positions = lax.broadcasted_iota(jnp.int32, (seqs_here, seq_len), 1)
    valid = (positions < valid_lengths[:, None]).astype(jnp.float32)
    own_gaps = jnp.sum(gap_of_token.reshape(seqs_here, seq_len) * valid, axis=1)
    gaps = spread(own_gaps, ("zh", "x", "c"), 16).reshape(-1)

    total_seqs = gaps.shape[0]
    pair_count = pair_rows.shape[0]
    row_ids = lax.broadcasted_iota(jnp.int32, (pair_count, total_seqs), 1)
    signs = (row_ids == pair_rows[:, 0:1]).astype(jnp.float32) - (
        row_ids == pair_rows[:, 1:2]
    ).astype(jnp.float32)
    margins = beta_scale * jnp.sum(signs * gaps[None, :], axis=1)
    loss = jnp.sum(jax.nn.softplus(-margins))
    slopes = -jax.nn.sigmoid(-margins)
    own_ids = lax.axis_index(("zh", "x", "c")) * seqs_here + lax.broadcasted_iota(
        jnp.int32, (1, seqs_here), 1
    )
    own_chosen = (pair_rows[:, 0:1] == own_ids).astype(jnp.float32)
    own_rejected = (pair_rows[:, 1:2] == own_ids).astype(jnp.float32)
    coef = beta_scale * jnp.sum(slopes[:, None] * (own_chosen - own_rejected), axis=0)
    token_coef = (coef[:, None] * valid).reshape(tokens_here)
    step_size = token_coef * policy_scale
    correction = policy_dotted * policy_scale * policy_scale / D
    hidden_grad = (
        step_size[None, None, :]
        * (
            all_gain[:, :, None] * all_targets.astype(jnp.float32)
            - all_hidden.astype(jnp.float32) * correction[None, None, :]
        )
    ).astype(jnp.bfloat16)

    grad = lax.dot_general(
        hidden_grad.reshape(NY * rows, tokens_here),
        policy_columns,
        (((1,), (0,)), ((), ())),
        preferred_element_type=jnp.float32,
    )
    grad = grad.reshape(NY * rows, 2, 2, 256)
    other = lax.dynamic_index_in_dim(grad, 1 - core, 2, keepdims=False)
    mine = lax.dynamic_index_in_dim(grad, core, 2, keepdims=False)
    grad = mine + lax.ppermute(other, "c", swap(2, 1))
    grad = grad.reshape(NY * rows, 2, 2, 128).transpose(2, 1, 0, 3).reshape(NX, NY * rows, 128)
    grad = jnp.sum(lax.all_to_all(grad, "x", 0, 0), axis=0)
    grad = lax.all_to_all(grad.reshape(NY, rows, 128), "y", 0, 0).reshape(2, 2, rows, 128)
    other = lax.dynamic_index_in_dim(grad, 1 - z_hi, 0, keepdims=False)
    mine = lax.dynamic_index_in_dim(grad, z_hi, 0, keepdims=False)
    grad = mine + lax.ppermute(other, "zh", swap(2, 1))
    half = x // 2
    other = lax.dynamic_index_in_dim(grad, 1 - half, 0, keepdims=False)
    mine = lax.dynamic_index_in_dim(grad, half, 0, keepdims=False)
    other = lax.ppermute(other, "x", swap(NX, 2))
    first = jnp.where(half == 0, mine, other)
    second = jnp.where(half == 0, other, mine)
    weight_grad = jnp.concatenate([first, second], axis=1)
    return (weight_grad, margins, loss)


def solution(mesh):
    dp, blk = ("zh", "x", "c"), ("y", "zl")
    fine = Mesh(mesh.devices.reshape(2, 4, 2, 4, 8), dp + blk)
    placed = (
        P(dp, blk),
        P(dp, blk),
        P(blk, dp),
        P(blk, dp),
        P(blk, dp),
        P(blk),
        P(blk),
        P(blk, None),
        P(blk, None),
        P(dp),
        P(),
    )
    return jax.shard_map(
        shards, mesh=fine, in_specs=placed, out_specs=(P(blk, dp), P(), P()), check_vma=False
    )
```

```python
import jax
import jax.numpy as jnp
from jax import lax
from jax.sharding import Mesh, PartitionSpec as P

D = 4608
NX, NY, NZ = 4, 4, 8

beta_scale = 0.1
epsilon = 1e-06


def spread(value, axes, count):
    return lax.all_to_all(jnp.broadcast_to(value[None], (count,) + value.shape), axes, 0, 0)


def swapped(value, axis):
    return lax.ppermute(value, axis, [(0, 1), (1, 0)])


def rows_of_all_y(weight, core):
    rows, features = weight.shape
    half = weight.reshape(rows, NY, 2, NZ // 2, 128)
    half = lax.dynamic_index_in_dim(half, core, 2, keepdims=False)
    half = half.transpose(0, 2, 1, 3).reshape(rows, features // 2)
    mine = spread(half, "y", NY).reshape(NY * rows, features // 2)
    halves = jnp.broadcast_to(mine[None], (2,) + mine.shape)
    return lax.dynamic_update_index_in_dim(halves, swapped(mine, "c"), 1 - core, 0)


def hidden_of(weight, context, stream):
    depth = weight.shape[2]
    for half in range(2):
        stream = stream.astype(jnp.float32) + lax.dot_general(
            weight[half],
            context[:, half * depth : (half + 1) * depth],
            (((1,), (1,)), ((), ())),
            preferred_element_type=jnp.float32,
        )
    return stream


def shards(
    policy_context,
    frozen_context,
    policy_stream,
    frozen_stream,
    targets,
    policy_gain,
    frozen_gain,
    policy_weight,
    frozen_weight,
    valid_lengths,
    pair_rows,
):
    rows, tokens_here = policy_stream.shape
    seq_len = tokens_here // valid_lengths.shape[0]
    seqs = valid_lengths.shape[0] // NY
    tokens = tokens_here // NY
    z_hi, core, y = lax.axis_index("zh"), lax.axis_index("c"), lax.axis_index("y")

    contexts = jnp.stack(
        [policy_context.reshape(NY, tokens, 128), frozen_context.reshape(NY, tokens, 128)], axis=1
    )
    contexts = lax.all_to_all(contexts, "y", 0, 0)
    contexts = contexts.transpose(1, 2, 0, 3).reshape(2 * tokens, NY * 128)
    contexts = lax.all_gather(contexts, "zl", axis=1, tiled=True)

    frozen_rows = rows_of_all_y(frozen_weight, core)
    policy_rows = rows_of_all_y(policy_weight, core)
    streams = jnp.stack(
        [
            s.reshape(rows, NY, tokens).transpose(1, 0, 2)
            for s in (policy_stream, frozen_stream, targets)
        ],
        axis=1,
    )
    streams = lax.all_to_all(streams, "y", 0, 0)
    streams = [streams[:, i].reshape(NY * rows, tokens) for i in range(3)]
    gains = spread(jnp.stack([policy_gain, frozen_gain]), "y", NY)
    gains = [gains[:, i].reshape(NY * rows, 1) for i in range(2)]
    contexts, frozen_rows, policy_rows, streams, gains = lax.optimization_barrier(
        (contexts, frozen_rows, policy_rows, streams, gains)
    )

    policy_columns, frozen_columns = contexts[:tokens], contexts[tokens:]
    frozen_hidden = hidden_of(frozen_rows, frozen_columns, streams[1])
    policy_hidden = hidden_of(policy_rows, policy_columns, streams[0])
    target_values = streams[2].astype(jnp.float32)
    policy_weighted = gains[0] * target_values
    frozen_weighted = gains[1] * target_values
    stats = jnp.stack(
        [
            jnp.sum(policy_hidden * policy_hidden, axis=0),
            jnp.sum(policy_hidden * policy_weighted, axis=0),
            jnp.sum(frozen_hidden * frozen_hidden, axis=0),
            jnp.sum(frozen_hidden * frozen_weighted, axis=0),
        ]
    )
    stats = jnp.sum(spread(stats, "zl", NZ), axis=0)

    policy_scale = lax.rsqrt(stats[0] / D + epsilon)
    frozen_scale = lax.rsqrt(stats[2] / D + epsilon)
    policy_dotted = stats[1]
    gap_of_token = policy_scale * policy_dotted - frozen_scale * stats[3]
    lengths = lax.dynamic_slice_in_dim(valid_lengths, y * seqs, seqs, 0)
    positions = lax.broadcasted_iota(jnp.int32, (seqs, seq_len), 1)
    valid = (positions < lengths[:, None]).astype(jnp.float32)
    own_gaps = jnp.sum(gap_of_token.reshape(seqs, seq_len) * valid, axis=1)
    other_gaps = swapped(own_gaps, "c")
    chip_gaps = jnp.where(
        core == 0, jnp.stack([own_gaps, other_gaps]), jnp.stack([other_gaps, own_gaps])
    )
    gaps = spread(chip_gaps, ("zh", "x", "y"), 2 * NX * NY)
    gaps = gaps.reshape(2 * NX, NY, 2, seqs).transpose(0, 2, 1, 3).reshape(-1)

    total_seqs = gaps.shape[0]
    pair_count = pair_rows.shape[0]
    row_ids = lax.broadcasted_iota(jnp.int32, (pair_count, total_seqs), 1)
    signs = (row_ids == pair_rows[:, 0:1]).astype(jnp.float32) - (
        row_ids == pair_rows[:, 1:2]
    ).astype(jnp.float32)
    margins = beta_scale * jnp.sum(signs * gaps[None, :], axis=1)
    loss = jnp.sum(jax.nn.softplus(-margins))
    slopes = -jax.nn.sigmoid(-margins)
    own_ids = (
        (lax.axis_index(("zh", "x", "c")) * NY + y) * seqs
        + lax.broadcasted_iota(jnp.int32, (1, seqs), 1)
    )
    own_chosen = (pair_rows[:, 0:1] == own_ids).astype(jnp.float32)
    own_rejected = (pair_rows[:, 1:2] == own_ids).astype(jnp.float32)
    coef = beta_scale * jnp.sum(slopes[:, None] * (own_chosen - own_rejected), axis=0)
    token_coef = (coef[:, None] * valid).reshape(tokens)
    step_size = token_coef * policy_scale
    correction = policy_dotted * policy_scale * policy_scale / D
    hidden_grad = (
        step_size[None, :] * (policy_weighted - policy_hidden * correction[None, :])
    ).astype(jnp.bfloat16)

    columns = policy_columns.reshape(tokens, 2, 2, 2, 2, 2, 128).transpose(2, 4, 0, 5, 1, 3, 6)
    columns = columns.reshape(4, tokens, NX, 256)

    def grad_of(core, z_hi):
        piece = lax.dynamic_index_in_dim(columns, 2 * core + z_hi, 0, keepdims=False)
        return lax.dot_general(
            hidden_grad, piece, (((1,), (0,)), ((), ())), preferred_element_type=jnp.float32
        ).transpose(1, 0, 2)

    z_order = (1 - z_hi, z_hi)
    arrived = [swapped(grad_of(1 - core, z).astype(jnp.bfloat16), "c") for z in z_order]
    sums = []
    for z, piece in zip(z_order, arrived):
        grad = (grad_of(core, z) + piece.astype(jnp.float32)).astype(jnp.bfloat16)
        grad = lax.all_to_all(grad.reshape(NX * NY, rows, 256), ("x", "y"), 0, 0)
        sums.append(jnp.sum(grad.astype(jnp.float32), axis=0))
    weight_grad = sums[1] + swapped(sums[0], "zh")
    return (weight_grad, margins, loss)


def solution(mesh):
    dp, blk = ("zh", "x", "c"), ("y", "zl")
    fine = Mesh(mesh.devices.reshape(2, NX, 2, NY, NZ), dp + blk)
    placed = (
        P(dp, blk),
        P(dp, blk),
        P(blk, dp),
        P(blk, dp),
        P(blk, dp),
        P(blk),
        P(blk),
        P(blk, None),
        P(blk, None),
        P(dp),
        P(),
    )
    return jax.shard_map(
        shards, mesh=fine, in_specs=placed, out_specs=(P(blk, dp), P(), P()), check_vma=False
    )
```

```python
import jax
import jax.numpy as jnp
from jax import lax
from jax.experimental import pallas as pl
from jax.experimental.pallas import tpu as pltpu
from jax.sharding import Mesh, PartitionSpec as P

D = 4608
NX, NY, NZ = 4, 4, 8

beta_scale = 0.1
epsilon = 1e-06


def spread(value, axes, count):
    return lax.all_to_all(jnp.broadcast_to(value[None], (count,) + value.shape), axes, 0, 0)


def swapped(value, axis):
    return lax.ppermute(value, axis, [(0, 1), (1, 0)])


def rows_of_all_y(weight, core):
    rows, features = weight.shape
    half = lax.dynamic_slice_in_dim(weight, core * (rows // 2), rows // 2, 0)
    half = half.reshape(rows // 2, NY, NZ, 128).transpose(0, 2, 1, 3).reshape(rows // 2, features)
    mine = spread(half, "y", NY).reshape(NY * rows // 2, features)
    return mine, swapped(mine, "c")


def own_first(value, core):
    return [
        lax.dynamic_index_in_dim(value, i, 1, keepdims=False).reshape(-1, value.shape[-1])
        for i in (core, 1 - core)
    ]


def forward_step(
    core_ref,
    context_ref,
    policy_mine_ref,
    policy_other_ref,
    frozen_mine_ref,
    frozen_other_ref,
    policy_stream_ref,
    frozen_stream_ref,
    targets_ref,
    gains_ref,
    hidden_ref,
    stats_ref,
    own_columns_ref,
    other_columns_ref,
    frozen_ref,
):
    step = pl.program_id(0)
    tokens = hidden_ref.shape[2]

    @pl.when(step == 0)
    def _():
        hidden_ref[...] = policy_stream_ref[...].astype(jnp.float32)
        frozen_ref[...] = frozen_stream_ref[...].astype(jnp.float32)

    policy_context = context_ref[:tokens, :]
    frozen_context = context_ref[tokens:, :]
    for sums, half, weight, context in (
        (hidden_ref, 0, policy_mine_ref, policy_context),
        (hidden_ref, 1, policy_other_ref, policy_context),
        (frozen_ref, 0, frozen_mine_ref, frozen_context),
        (frozen_ref, 1, frozen_other_ref, frozen_context),
    ):
        sums[half] += lax.dot_general(
            weight[...], context, (((1,), (1,)), ((), ())), preferred_element_type=jnp.float32
        )

    def move(columns_ref):
        for i in range(2 * NY):
            e, y = i // NY, i % NY
            columns_ref[y // 2, 2 * (y % 2) + lax.div(step, 2), :, e * 128 : (e + 1) * 128] = (
                context_ref[:tokens, i * 128 : (i + 1) * 128]
            )

    @pl.when(lax.rem(step, 2) == core_ref[0])
    def _():
        move(own_columns_ref)

    @pl.when(lax.rem(step, 2) != core_ref[0])
    def _():
        move(other_columns_ref)

    @pl.when(step == NZ // 2 - 1)
    def _():
        totals = [0.0] * 4
        for half in range(2):
            target = targets_ref[half].astype(jnp.float32)
            for model, hidden in enumerate((hidden_ref[half], frozen_ref[half])):
                gain = gains_ref[:, 2 * model + half : 2 * model + half + 1]
                terms = (hidden * hidden, hidden * (gain * target))
                for i, term in enumerate(terms):
                    totals[2 * model + i] += jnp.sum(term, axis=0, keepdims=True)
        for i in range(4):
            stats_ref[:, i : i + 1, :] = jnp.broadcast_to(totals[i][None], (NZ, 1, tokens))


def forward(core, contexts, policy_rows, frozen_rows, streams, gains):
    half_rows, features = policy_rows[0].shape
    tokens = contexts.shape[0] // 2
    depth = features // (NZ // 2)

    def whole(*shape):
        return pl.BlockSpec(shape, lambda z: (0,) * len(shape))

    weight = pl.BlockSpec((half_rows, depth), lambda z: (0, z))
    block = (2, half_rows, tokens)
    columns = (2, NX, tokens, 256)
    return pl.pallas_call(
        forward_step,
        grid=(NZ // 2,),
        in_specs=[
            pl.BlockSpec(memory_space=pltpu.SMEM),
            pl.BlockSpec((2 * tokens, depth), lambda z: (0, z)),
            weight,
            weight,
            weight,
            weight,
            whole(*block),
            whole(*block),
            whole(*block),
            whole(half_rows, 4),
        ],
        out_specs=[whole(*block), whole(NZ, 4, tokens), whole(*columns), whole(*columns)],
        out_shape=[
            jax.ShapeDtypeStruct(block, jnp.float32),
            jax.ShapeDtypeStruct((NZ, 4, tokens), jnp.float32),
            jax.ShapeDtypeStruct(columns, jnp.bfloat16),
            jax.ShapeDtypeStruct(columns, jnp.bfloat16),
        ],
        scratch_shapes=[pltpu.VMEM(block, jnp.float32)],
        compiler_params=pltpu.CompilerParams(vmem_limit_bytes=56 * 2**20),
        cost_estimate=pl.CostEstimate(
            flops=8 * half_rows * tokens * features,
            bytes_accessed=2 * features * (4 * half_rows + 3 * tokens),
            transcendentals=0,
        ),
    )(core[None], contexts, *policy_rows, *frozen_rows, *streams, gains)


def shards(
    policy_context,
    frozen_context,
    policy_stream,
    frozen_stream,
    targets,
    policy_gain,
    frozen_gain,
    policy_weight,
    frozen_weight,
    valid_lengths,
    pair_rows,
):
    rows, tokens_here = policy_stream.shape
    seq_len = tokens_here // valid_lengths.shape[0]
    seqs = valid_lengths.shape[0] // NY
    tokens = tokens_here // NY
    z_hi, core, y = lax.axis_index("zh"), lax.axis_index("c"), lax.axis_index("y")

    contexts = jnp.stack(
        [policy_context.reshape(NY, tokens, 128), frozen_context.reshape(NY, tokens, 128)], axis=1
    )
    contexts = lax.all_to_all(contexts, "y", 0, 0)
    contexts = contexts.transpose(1, 2, 0, 3).reshape(2 * tokens, NY * 128)
    contexts = lax.all_gather(contexts, "zl", axis=1, tiled=True)

    frozen_rows = rows_of_all_y(frozen_weight, core)
    policy_rows = rows_of_all_y(policy_weight, core)
    streams = jnp.stack(
        [
            s.reshape(rows, NY, tokens).transpose(1, 0, 2)
            for s in (policy_stream, frozen_stream, targets)
        ],
        axis=1,
    )
    streams = lax.all_to_all(streams, "y", 0, 0)
    streams = streams.reshape(NY, 3, 2, rows // 2, tokens)
    streams = [jnp.stack(own_first(streams[:, i], core)) for i in range(3)]
    gains = spread(jnp.stack([policy_gain, frozen_gain]), "y", NY)
    gains = gains.reshape(NY, 2, 2, rows // 2, 1)
    gains = jnp.concatenate([g for i in range(2) for g in own_first(gains[:, i], core)], axis=1)
    other_targets = swapped(streams[2], "c")
    contexts, frozen_rows, policy_rows, streams, gains, other_targets = lax.optimization_barrier(
        (contexts, frozen_rows, policy_rows, streams, gains, other_targets)
    )

    policy_hidden, stats, columns, other_columns = forward(
        core, contexts, policy_rows, frozen_rows, streams, gains
    )
    stats = jnp.sum(lax.all_to_all(stats, "zl", 0, 0), axis=0)
    other_hidden = swapped(policy_hidden, "c")
    other_columns = swapped(other_columns, "c")

    policy_scale = lax.rsqrt(stats[0] / D + epsilon)
    frozen_scale = lax.rsqrt(stats[2] / D + epsilon)
    policy_dotted = stats[1]
    gap_of_token = policy_scale * policy_dotted - frozen_scale * stats[3]
    lengths = lax.dynamic_slice_in_dim(valid_lengths, y * seqs, seqs, 0)
    positions = lax.broadcasted_iota(jnp.int32, (seqs, seq_len), 1)
    valid = (positions < lengths[:, None]).astype(jnp.float32)
    own_gaps = jnp.sum(gap_of_token.reshape(seqs, seq_len) * valid, axis=1)
    told = jnp.concatenate([own_gaps, policy_scale, policy_dotted, valid.reshape(-1)])
    other_told = swapped(told, "c")
    other_gaps, other_told = other_told[:seqs], other_told[seqs:].reshape(3, tokens)
    chip_gaps = jnp.where(
        core == 0, jnp.stack([own_gaps, other_gaps]), jnp.stack([other_gaps, own_gaps])
    )
    gaps = spread(chip_gaps, ("zh", "x", "y"), 2 * NX * NY)
    gaps, other_columns, other_hidden = lax.optimization_barrier(
        (gaps, other_columns, other_hidden)
    )
    gaps = gaps.reshape(2 * NX, NY, 2, seqs).transpose(0, 2, 1, 3).reshape(-1)

    total_seqs = gaps.shape[0]
    pair_count = pair_rows.shape[0]
    row_ids = lax.broadcasted_iota(jnp.int32, (pair_count, total_seqs), 1)
    signs = (row_ids == pair_rows[:, 0:1]).astype(jnp.float32) - (
        row_ids == pair_rows[:, 1:2]
    ).astype(jnp.float32)
    margins = beta_scale * jnp.sum(signs * gaps[None, :], axis=1)
    loss = jnp.sum(jax.nn.softplus(-margins))
    slopes = -jax.nn.sigmoid(-margins)

    policy_gain = gains[:, :2].T[:, :, None]

    def hidden_grad_of(core_of_tokens, scale, dotted, valid, gain, all_targets, all_hidden):
        own_ids = (
            ((lax.axis_index(("zh", "x")) * 2 + core_of_tokens) * NY + y) * seqs
            + lax.broadcasted_iota(jnp.int32, (1, seqs), 1)
        )
        own_chosen = (pair_rows[:, 0:1] == own_ids).astype(jnp.float32)
        own_rejected = (pair_rows[:, 1:2] == own_ids).astype(jnp.float32)
        coef = beta_scale * jnp.sum(slopes[:, None] * (own_chosen - own_rejected), axis=0)
        step_size = jnp.broadcast_to(coef[:, None], (seqs, seq_len)).reshape(tokens) * valid * scale
        correction = dotted * scale * scale / D
        grad = step_size * (gain * all_targets.astype(jnp.float32) - all_hidden * correction)
        grad = grad.astype(jnp.bfloat16)
        grad = jnp.where(core_of_tokens == 0, grad, grad[::-1]).reshape(2, NY, rows // 2, tokens)
        return grad.transpose(1, 0, 2, 3).reshape(NY * rows, tokens)

    own_grad = hidden_grad_of(
        core,
        policy_scale,
        policy_dotted,
        valid.reshape(-1),
        policy_gain,
        streams[2],
        policy_hidden,
    )
    other_grad = hidden_grad_of(
        1 - core, *other_told, policy_gain[::-1], other_targets, other_hidden
    )
    hidden_grad = jnp.concatenate([own_grad, other_grad], axis=1)
    columns = jnp.concatenate([columns, other_columns], axis=2)

    def grad_of(z_hi):
        piece = lax.dynamic_index_in_dim(columns, z_hi, 0, keepdims=False)
        return jnp.stack(
            [jnp.dot(hidden_grad, piece[i], preferred_element_type=jnp.float32) for i in range(NX)]
        )

    z_order = (1 - z_hi, z_hi)
    sums = []
    for z in z_order:
        grad = grad_of(z).astype(jnp.bfloat16).reshape(NX * NY, rows, 256)
        grad = lax.all_to_all(grad, ("x", "y"), 0, 0)
        sums.append(jnp.sum(grad.astype(jnp.float32), axis=0))
    weight_grad = sums[1] + swapped(sums[0], "zh")
    return (weight_grad, margins, loss)


def solution(mesh):
    dp, blk = ("zh", "x", "c"), ("y", "zl")
    fine = Mesh(mesh.devices.reshape(2, NX, 2, NY, NZ), dp + blk)
    placed = (
        P(dp, blk),
        P(dp, blk),
        P(blk, dp),
        P(blk, dp),
        P(blk, dp),
        P(blk),
        P(blk),
        P(blk, None),
        P(blk, None),
        P(dp),
        P(),
    )
    return jax.shard_map(
        shards, mesh=fine, in_specs=placed, out_specs=(P(blk, dp), P(), P()), check_vma=False
    )
```

```python
import jax
import jax.numpy as jnp
from jax import lax
from jax.experimental import pallas as pl
from jax.experimental.pallas import tpu as pltpu
from jax.sharding import Mesh, PartitionSpec as P

D = 4608
NX, NY, NZ = 4, 4, 8

beta_scale = 0.1
epsilon = 1e-06


def spread(value, axes, count):
    return lax.all_to_all(jnp.broadcast_to(value[None], (count,) + value.shape), axes, 0, 0)


def swapped(value, axis):
    return lax.ppermute(value, axis, [(0, 1), (1, 0)])


def rows_of_all_y(weight, core):
    rows, features = weight.shape
    half = lax.dynamic_slice_in_dim(weight, core * (rows // 2), rows // 2, 0)
    half = half.reshape(rows // 2, NY, NZ, 128).transpose(0, 2, 1, 3).reshape(rows // 2, features)
    mine = spread(half, "y", NY).reshape(NY * rows // 2, features)
    return mine, swapped(mine, "c")


def own_first(value, core):
    return [
        lax.dynamic_index_in_dim(value, i, 1, keepdims=False).reshape(-1, value.shape[-1])
        for i in (core, 1 - core)
    ]


def forward_step(
    core_ref,
    context_ref,
    policy_mine_ref,
    policy_other_ref,
    frozen_mine_ref,
    frozen_other_ref,
    policy_stream_ref,
    frozen_stream_ref,
    targets_ref,
    gains_ref,
    valid_ref,
    hidden_ref,
    stats_ref,
    own_columns_ref,
    other_columns_ref,
    frozen_ref,
):
    step = pl.program_id(0)
    tokens = hidden_ref.shape[2]

    @pl.when(step == 0)
    def _():
        hidden_ref[...] = policy_stream_ref[...].astype(jnp.float32)
        frozen_ref[...] = frozen_stream_ref[...].astype(jnp.float32)

    policy_context = context_ref[:tokens, :]
    frozen_context = context_ref[tokens:, :]
    for sums, half, weight, context in (
        (hidden_ref, 0, policy_mine_ref, policy_context),
        (hidden_ref, 1, policy_other_ref, policy_context),
        (frozen_ref, 0, frozen_mine_ref, frozen_context),
        (frozen_ref, 1, frozen_other_ref, frozen_context),
    ):
        sums[half] += lax.dot_general(
            weight[...], context, (((1,), (1,)), ((), ())), preferred_element_type=jnp.float32
        )

    def move(columns_ref):
        for i in range(2 * NY):
            e, y = i // NY, i % NY
            columns_ref[y // 2, 2 * (y % 2) + lax.div(step, 2), :, e * 128 : (e + 1) * 128] = (
                context_ref[:tokens, i * 128 : (i + 1) * 128]
            )

    @pl.when(lax.rem(step, 2) == core_ref[0])
    def _():
        move(own_columns_ref)

    @pl.when(lax.rem(step, 2) != core_ref[0])
    def _():
        move(other_columns_ref)

    @pl.when(step == NZ // 2 - 1)
    def _():
        totals = [0.0] * 4
        for half in range(2):
            target = targets_ref[half].astype(jnp.float32)
            for model, hidden in enumerate((hidden_ref[half], frozen_ref[half])):
                gain = gains_ref[:, 2 * model + half : 2 * model + half + 1]
                terms = (hidden * hidden, hidden * (gain * target))
                for i, term in enumerate(terms):
                    totals[2 * model + i] += jnp.sum(term, axis=0, keepdims=True)
        totals.append(valid_ref[...])
        for i in range(5):
            stats_ref[:, i : i + 1, :] = jnp.broadcast_to(
                totals[i][None], (2 * NZ, 1, tokens)
            )


def forward(core, contexts, policy_rows, frozen_rows, streams, gains, valid):
    half_rows, features = policy_rows[0].shape
    tokens = contexts.shape[0] // 2
    depth = features // (NZ // 2)

    def whole(*shape):
        return pl.BlockSpec(shape, lambda z: (0,) * len(shape))

    weight = pl.BlockSpec((half_rows, depth), lambda z: (0, z))
    block = (2, half_rows, tokens)
    columns = (2, NX, tokens, 256)
    return pl.pallas_call(
        forward_step,
        grid=(NZ // 2,),
        in_specs=[
            pl.BlockSpec(memory_space=pltpu.SMEM),
            pl.BlockSpec((2 * tokens, depth), lambda z: (0, z)),
            weight,
            weight,
            weight,
            weight,
            whole(*block),
            whole(*block),
            whole(*block),
            whole(half_rows, 4),
            whole(1, tokens),
        ],
        out_specs=[whole(*block), whole(2 * NZ, 5, tokens), whole(*columns), whole(*columns)],
        out_shape=[
            jax.ShapeDtypeStruct(block, jnp.float32),
            jax.ShapeDtypeStruct((2 * NZ, 5, tokens), jnp.float32),
            jax.ShapeDtypeStruct(columns, jnp.bfloat16),
            jax.ShapeDtypeStruct(columns, jnp.bfloat16),
        ],
        scratch_shapes=[pltpu.VMEM(block, jnp.float32)],
        compiler_params=pltpu.CompilerParams(vmem_limit_bytes=56 * 2**20),
        cost_estimate=pl.CostEstimate(
            flops=8 * half_rows * tokens * features,
            bytes_accessed=2 * features * (4 * half_rows + 3 * tokens),
            transcendentals=0,
        ),
    )(core[None], contexts, *policy_rows, *frozen_rows, *streams, gains, valid)


def shards(
    policy_context,
    frozen_context,
    policy_stream,
    frozen_stream,
    targets,
    policy_gain,
    frozen_gain,
    policy_weight,
    frozen_weight,
    valid_lengths,
    pair_rows,
):
    rows, tokens_here = policy_stream.shape
    seq_len = tokens_here // valid_lengths.shape[0]
    seqs = valid_lengths.shape[0] // NY
    tokens = tokens_here // NY
    z_hi, core, y = lax.axis_index("zh"), lax.axis_index("c"), lax.axis_index("y")

    contexts = jnp.stack(
        [policy_context.reshape(NY, tokens, 128), frozen_context.reshape(NY, tokens, 128)], axis=1
    )
    contexts = lax.all_to_all(contexts, "y", 0, 0)
    contexts = contexts.transpose(1, 2, 0, 3).reshape(2 * tokens, NY * 128)
    contexts = lax.all_gather(contexts, "zl", axis=1, tiled=True)

    frozen_rows = rows_of_all_y(frozen_weight, core)
    policy_rows = rows_of_all_y(policy_weight, core)
    streams = jnp.stack(
        [
            s.reshape(rows, NY, tokens).transpose(1, 0, 2)
            for s in (policy_stream, frozen_stream, targets)
        ],
        axis=1,
    )
    streams = lax.all_to_all(streams, "y", 0, 0)
    streams = streams.reshape(NY, 3, 2, rows // 2, tokens)
    streams = [jnp.stack(own_first(streams[:, i], core)) for i in range(3)]
    gains = spread(jnp.stack([policy_gain, frozen_gain]), "y", NY)
    gains = gains.reshape(NY, 2, 2, rows // 2, 1)
    gains = jnp.concatenate([g for i in range(2) for g in own_first(gains[:, i], core)], axis=1)
    other_targets = swapped(streams[2], "c")
    lengths = lax.dynamic_slice_in_dim(valid_lengths, y * seqs, seqs, 0)
    positions = lax.broadcasted_iota(jnp.int32, (seqs, seq_len), 1)
    valid = (positions < lengths[:, None]).astype(jnp.float32).reshape(1, tokens)
    contexts, frozen_rows, policy_rows, streams, gains, other_targets, valid = (
        lax.optimization_barrier(
            (contexts, frozen_rows, policy_rows, streams, gains, other_targets, valid)
        )
    )
    policy_hidden, stats, columns, other_columns = forward(
        core, contexts, policy_rows, frozen_rows, streams, gains, valid
    )
    stats = lax.all_to_all(stats, ("zh", "zl"), 0, 0).reshape(2, NZ, 5, tokens)
    valid = stats[:, 0, 4]
    stats = jnp.sum(stats[:, :, :4], axis=1)
    other_hidden = swapped(policy_hidden, "c")
    other_columns = swapped(other_columns, "c")

    scales = lax.rsqrt(stats[:, 0::2] / D + epsilon)
    gap_of_token = scales[:, 0] * stats[:, 1] - scales[:, 1] * stats[:, 3]
    own_gaps = jnp.sum((gap_of_token * valid).reshape(2 * seqs, seq_len), axis=1)
    scalars = jnp.stack([scales[:, 0], stats[:, 1], valid], axis=1)
    scalars = lax.dynamic_index_in_dim(scalars, z_hi, 0, keepdims=False)
    told = jnp.concatenate([own_gaps, scalars.reshape(-1)])
    other_told = swapped(told, "c")
    other_gaps, other_told = other_told[: 2 * seqs], other_told[2 * seqs :].reshape(3, tokens)
    chip_gaps = jnp.where(
        core == 0, jnp.stack([own_gaps, other_gaps]), jnp.stack([other_gaps, own_gaps])
    )
    gaps = spread(chip_gaps, ("x", "y"), NX * NY)
    gaps, other_columns, other_hidden = lax.optimization_barrier(
        (gaps, other_columns, other_hidden)
    )
    gaps = gaps.reshape(NX, NY, 2, 2, seqs).transpose(3, 0, 2, 1, 4).reshape(-1)

    total_seqs = gaps.shape[0]
    pair_count = pair_rows.shape[0]
    row_ids = lax.broadcasted_iota(jnp.int32, (pair_count, total_seqs), 1)
    signs = (row_ids == pair_rows[:, 0:1]).astype(jnp.float32) - (
        row_ids == pair_rows[:, 1:2]
    ).astype(jnp.float32)
    margins = beta_scale * jnp.sum(signs * gaps[None, :], axis=1)
    loss = jnp.sum(jax.nn.softplus(-margins))
    slopes = -jax.nn.sigmoid(-margins)

    policy_gain = gains[:, :2].T[:, :, None]

    def hidden_grad_of(core_of_tokens, scale, dotted, valid, gain, all_targets, all_hidden):
        own_ids = (
            ((lax.axis_index(("zh", "x")) * 2 + core_of_tokens) * NY + y) * seqs
            + lax.broadcasted_iota(jnp.int32, (1, seqs), 1)
        )
        own_chosen = (pair_rows[:, 0:1] == own_ids).astype(jnp.float32)
        own_rejected = (pair_rows[:, 1:2] == own_ids).astype(jnp.float32)
        coef = beta_scale * jnp.sum(slopes[:, None] * (own_chosen - own_rejected), axis=0)
        step_size = jnp.broadcast_to(coef[:, None], (seqs, seq_len)).reshape(tokens) * valid * scale
        correction = dotted * scale * scale / D
        grad = step_size * (gain * all_targets.astype(jnp.float32) - all_hidden * correction)
        grad = grad.astype(jnp.bfloat16)
        grad = jnp.where(core_of_tokens == 0, grad, grad[::-1]).reshape(2, NY, rows // 2, tokens)
        return grad.transpose(1, 0, 2, 3).reshape(NY * rows, tokens)

    own_grad = hidden_grad_of(core, *scalars, policy_gain, streams[2], policy_hidden)
    other_grad = hidden_grad_of(
        1 - core, *other_told, policy_gain[::-1], other_targets, other_hidden
    )
    hidden_grad = jnp.concatenate([own_grad, other_grad], axis=1)
    columns = jnp.concatenate([columns, other_columns], axis=2)

    def grad_of(z_hi):
        piece = lax.dynamic_index_in_dim(columns, z_hi, 0, keepdims=False)
        return jnp.stack(
            [jnp.dot(hidden_grad, piece[i], preferred_element_type=jnp.float32) for i in range(NX)]
        )

    z_order = (1 - z_hi, z_hi)
    sums = []
    for z in z_order:
        grad = grad_of(z).astype(jnp.bfloat16).reshape(NX * NY, rows, 256)
        grad = lax.all_to_all(grad, ("x", "y"), 0, 0)
        sums.append(jnp.sum(grad.astype(jnp.float32), axis=0))
    weight_grad = sums[1] + swapped(sums[0], "zh")
    return (weight_grad, margins, loss)


def solution(mesh):
    dp, blk = ("zh", "x", "c"), ("y", "zl")
    fine = Mesh(mesh.devices.reshape(2, NX, 2, NY, NZ), dp + blk)
    placed = (
        P(dp, blk),
        P(dp, blk),
        P(blk, dp),
        P(blk, dp),
        P(blk, dp),
        P(blk),
        P(blk),
        P(blk, None),
        P(blk, None),
        P(dp),
        P(),
    )
    return jax.shard_map(
        shards, mesh=fine, in_specs=placed, out_specs=(P(blk, dp), P(), P()), check_vma=False
    )
```

```python
import jax
import jax.numpy as jnp
from jax import lax
from jax.experimental import pallas as pl
from jax.experimental.pallas import tpu as pltpu
from jax.sharding import Mesh, PartitionSpec as P

D = 4608
NX, NY, NZ = 4, 4, 8

beta_scale = 0.1
epsilon = 1e-06


def spread(value, axes, count):
    return lax.all_to_all(jnp.broadcast_to(value[None], (count,) + value.shape), axes, 0, 0)


def swapped(value, axis):
    return lax.ppermute(value, axis, [(0, 1), (1, 0)])


def rows_of_all_y(weight, core):
    rows, features = weight.shape
    half = lax.dynamic_slice_in_dim(weight, core * (rows // 2), rows // 2, 0)
    half = half.reshape(rows // 2, NY, NZ, 128).transpose(0, 2, 1, 3).reshape(rows // 2, features)
    mine = spread(half, "y", NY).reshape(NY * rows // 2, features)
    return mine, swapped(mine, "c")


def own_first(value, core):
    return [
        lax.dynamic_index_in_dim(value, i, 1, keepdims=False).reshape(-1, value.shape[-1])
        for i in (core, 1 - core)
    ]


def forward_step(
    core_ref,
    context_ref,
    policy_mine_ref,
    policy_other_ref,
    frozen_mine_ref,
    frozen_other_ref,
    policy_stream_ref,
    frozen_stream_ref,
    targets_ref,
    gains_ref,
    valid_ref,
    hidden_ref,
    stats_ref,
    own_columns_ref,
    other_columns_ref,
    frozen_ref,
):
    step = pl.program_id(0)
    tokens = hidden_ref.shape[2]

    @pl.when(step == 0)
    def _():
        hidden_ref[...] = policy_stream_ref[...].astype(jnp.float32)
        frozen_ref[...] = frozen_stream_ref[...].astype(jnp.float32)

    policy_context = context_ref[:tokens, :]
    frozen_context = context_ref[tokens:, :]
    for sums, half, weight, context in (
        (hidden_ref, 0, policy_mine_ref, policy_context),
        (hidden_ref, 1, policy_other_ref, policy_context),
        (frozen_ref, 0, frozen_mine_ref, frozen_context),
        (frozen_ref, 1, frozen_other_ref, frozen_context),
    ):
        sums[half] += lax.dot_general(
            weight[...], context, (((1,), (1,)), ((), ())), preferred_element_type=jnp.float32
        )

    def move(columns_ref):
        for i in range(2 * NY):
            e, y = i // NY, i % NY
            columns_ref[y // 2, 2 * (y % 2) + lax.div(step, 2), :, e * 128 : (e + 1) * 128] = (
                context_ref[:tokens, i * 128 : (i + 1) * 128]
            )

    @pl.when(lax.rem(step, 2) == core_ref[0])
    def _():
        move(own_columns_ref)

    @pl.when(lax.rem(step, 2) != core_ref[0])
    def _():
        move(other_columns_ref)

    @pl.when(step == NZ // 2 - 1)
    def _():
        totals = [0.0] * 4
        for half in range(2):
            target = targets_ref[half].astype(jnp.float32)
            for model, hidden in enumerate((hidden_ref[half], frozen_ref[half])):
                gain = gains_ref[:, 2 * model + half : 2 * model + half + 1]
                terms = (hidden * hidden, hidden * (gain * target))
                for i, term in enumerate(terms):
                    totals[2 * model + i] += jnp.sum(term, axis=0, keepdims=True)
        totals[1], totals[3] = totals[1] * valid_ref[...], totals[3] * valid_ref[...]
        for i in range(4):
            stats_ref[:, i : i + 1, :] = jnp.broadcast_to(
                totals[i][None], (2 * NZ, 1, tokens)
            )


def forward(core, contexts, policy_rows, frozen_rows, streams, gains, valid):
    half_rows, features = policy_rows[0].shape
    tokens = contexts.shape[0] // 2
    depth = features // (NZ // 2)

    def whole(*shape):
        return pl.BlockSpec(shape, lambda z: (0,) * len(shape))

    weight = pl.BlockSpec((half_rows, depth), lambda z: (0, z))
    block = (2, half_rows, tokens)
    columns = (2, NX, tokens, 256)
    return pl.pallas_call(
        forward_step,
        grid=(NZ // 2,),
        in_specs=[
            pl.BlockSpec(memory_space=pltpu.SMEM),
            pl.BlockSpec((2 * tokens, depth), lambda z: (0, z)),
            weight,
            weight,
            weight,
            weight,
            whole(*block),
            whole(*block),
            whole(*block),
            whole(half_rows, 4),
            whole(1, tokens),
        ],
        out_specs=[whole(*block), whole(2 * NZ, 4, tokens), whole(*columns), whole(*columns)],
        out_shape=[
            jax.ShapeDtypeStruct(block, jnp.float32),
            jax.ShapeDtypeStruct((2 * NZ, 4, tokens), jnp.float32),
            jax.ShapeDtypeStruct(columns, jnp.bfloat16),
            jax.ShapeDtypeStruct(columns, jnp.bfloat16),
        ],
        scratch_shapes=[pltpu.VMEM(block, jnp.float32)],
        compiler_params=pltpu.CompilerParams(vmem_limit_bytes=56 * 2**20),
        cost_estimate=pl.CostEstimate(
            flops=8 * half_rows * tokens * features,
            bytes_accessed=2 * features * (4 * half_rows + 3 * tokens),
            transcendentals=0,
        ),
    )(core[None], contexts, *policy_rows, *frozen_rows, *streams, gains, valid)


def shards(
    policy_context,
    frozen_context,
    policy_stream,
    frozen_stream,
    targets,
    policy_gain,
    frozen_gain,
    policy_weight,
    frozen_weight,
    valid_lengths,
    pair_rows,
):
    rows, tokens_here = policy_stream.shape
    seq_len = tokens_here // valid_lengths.shape[0]
    seqs = valid_lengths.shape[0] // NY
    tokens = tokens_here // NY
    z_hi, core, y = lax.axis_index("zh"), lax.axis_index("c"), lax.axis_index("y")

    contexts = jnp.stack(
        [policy_context.reshape(NY, tokens, 128), frozen_context.reshape(NY, tokens, 128)], axis=1
    )
    contexts = lax.all_to_all(contexts, "y", 0, 0)
    contexts = contexts.transpose(1, 2, 0, 3).reshape(2 * tokens, NY * 128)
    contexts = lax.all_gather(contexts, "zl", axis=1, tiled=True)

    frozen_rows = rows_of_all_y(frozen_weight, core)
    policy_rows = rows_of_all_y(policy_weight, core)
    streams = jnp.stack(
        [
            s.reshape(rows, NY, tokens).transpose(1, 0, 2)
            for s in (policy_stream, frozen_stream, targets)
        ],
        axis=1,
    )
    streams = lax.all_to_all(streams, "y", 0, 0)
    streams = streams.reshape(NY, 3, 2, rows // 2, tokens)
    streams = [jnp.stack(own_first(streams[:, i], core)) for i in range(3)]
    gains = spread(jnp.stack([policy_gain, frozen_gain]), "y", NY)
    gains = gains.reshape(NY, 2, 2, rows // 2, 1)
    gains = jnp.concatenate([g for i in range(2) for g in own_first(gains[:, i], core)], axis=1)
    other_targets = swapped(streams[2], "c")
    lengths = lax.dynamic_slice_in_dim(valid_lengths, y * seqs, seqs, 0)
    positions = lax.broadcasted_iota(jnp.int32, (seqs, seq_len), 1)
    valid = (positions < lengths[:, None]).astype(jnp.float32).reshape(1, tokens)
    contexts, frozen_rows, policy_rows, streams, gains, other_targets, valid = (
        lax.optimization_barrier(
            (contexts, frozen_rows, policy_rows, streams, gains, other_targets, valid)
        )
    )
    policy_hidden, stats, columns, other_columns = forward(
        core, contexts, policy_rows, frozen_rows, streams, gains, valid
    )
    stats = lax.all_to_all(stats, ("zh", "zl"), 0, 0).reshape(2, NZ, 4, tokens)
    stats = jnp.sum(stats, axis=1)
    other_hidden = swapped(policy_hidden, "c")
    other_columns = swapped(other_columns, "c")

    scales = lax.rsqrt(stats[:, 0::2] / D + epsilon)
    gap_of_token = scales[:, 0] * stats[:, 1] - scales[:, 1] * stats[:, 3]
    own_gaps = jnp.sum(gap_of_token.reshape(2 * seqs, seq_len), axis=1)
    scalars = jnp.stack([scales[:, 0], stats[:, 1]], axis=1)
    scalars = lax.dynamic_index_in_dim(scalars, z_hi, 0, keepdims=False)
    scalars = jnp.concatenate([scalars, valid])
    told = jnp.concatenate([own_gaps, scalars.reshape(-1)])
    other_told = swapped(told, "c")
    other_gaps, other_told = other_told[: 2 * seqs], other_told[2 * seqs :].reshape(3, tokens)
    chip_gaps = jnp.where(
        core == 0, jnp.stack([own_gaps, other_gaps]), jnp.stack([other_gaps, own_gaps])
    )
    gaps = spread(chip_gaps, ("x", "y"), NX * NY)
    gaps, other_columns, other_hidden = lax.optimization_barrier(
        (gaps, other_columns, other_hidden)
    )
    gaps = gaps.reshape(NX, NY, 2, 2, seqs).transpose(3, 0, 2, 1, 4).reshape(-1)

    total_seqs = gaps.shape[0]
    pair_count = pair_rows.shape[0]
    row_ids = lax.broadcasted_iota(jnp.int32, (pair_count, total_seqs), 1)
    signs = (row_ids == pair_rows[:, 0:1]).astype(jnp.float32) - (
        row_ids == pair_rows[:, 1:2]
    ).astype(jnp.float32)
    margins = beta_scale * jnp.sum(signs * gaps[None, :], axis=1)
    loss = jnp.sum(jax.nn.softplus(-margins))
    slopes = -jax.nn.sigmoid(-margins)

    policy_gain = gains[:, :2].T[:, :, None]

    def hidden_grad_of(core_of_tokens, scale, dotted, valid, gain, all_targets, all_hidden):
        own_ids = (
            ((lax.axis_index(("zh", "x")) * 2 + core_of_tokens) * NY + y) * seqs
            + lax.broadcasted_iota(jnp.int32, (1, seqs), 1)
        )
        own_chosen = (pair_rows[:, 0:1] == own_ids).astype(jnp.float32)
        own_rejected = (pair_rows[:, 1:2] == own_ids).astype(jnp.float32)
        coef = beta_scale * jnp.sum(slopes[:, None] * (own_chosen - own_rejected), axis=0)
        step_size = jnp.broadcast_to(coef[:, None], (seqs, seq_len)).reshape(tokens) * valid * scale
        correction = dotted * scale * scale / D
        grad = step_size * (gain * all_targets.astype(jnp.float32) - all_hidden * correction)
        grad = grad.astype(jnp.bfloat16)
        grad = jnp.where(core_of_tokens == 0, grad, grad[::-1]).reshape(2, NY, rows // 2, tokens)
        return grad.transpose(1, 0, 2, 3).reshape(NY * rows, tokens)

    own_grad = hidden_grad_of(core, *scalars, policy_gain, streams[2], policy_hidden)
    other_grad = hidden_grad_of(
        1 - core, *other_told, policy_gain[::-1], other_targets, other_hidden
    )
    hidden_grad = jnp.concatenate([own_grad, other_grad], axis=1)
    columns = jnp.concatenate([columns, other_columns], axis=2)

    def grad_of(z_hi):
        piece = lax.dynamic_index_in_dim(columns, z_hi, 0, keepdims=False)
        return jnp.stack(
            [jnp.dot(hidden_grad, piece[i], preferred_element_type=jnp.float32) for i in range(NX)]
        )

    z_order = (1 - z_hi, z_hi)
    sums = []
    for z in z_order:
        grad = grad_of(z).astype(jnp.bfloat16).reshape(NX * NY, rows, 256)
        grad = lax.all_to_all(grad, ("x", "y"), 0, 0)
        sums.append(jnp.sum(grad.astype(jnp.float32), axis=0))
    weight_grad = sums[1] + swapped(sums[0].astype(jnp.bfloat16), "zh").astype(jnp.float32)
    return (weight_grad, margins, loss)


def solution(mesh):
    dp, blk = ("zh", "x", "c"), ("y", "zl")
    fine = Mesh(mesh.devices.reshape(2, NX, 2, NY, NZ), dp + blk)
    placed = (
        P(dp, blk),
        P(dp, blk),
        P(blk, dp),
        P(blk, dp),
        P(blk, dp),
        P(blk),
        P(blk),
        P(blk, None),
        P(blk, None),
        P(dp),
        P(),
    )
    return jax.shard_map(
        shards, mesh=fine, in_specs=placed, out_specs=(P(blk, dp), P(), P()), check_vma=False
    )
```

```python
import jax
import jax.numpy as jnp
from jax import lax
from jax.experimental import pallas as pl
from jax.experimental.pallas import tpu as pltpu
from jax.sharding import Mesh, PartitionSpec as P

D = 4608
NX, NY, NZ = 4, 4, 8

beta_scale = 0.1
epsilon = 1e-06


def spread(value, axes, count):
    return lax.all_to_all(jnp.broadcast_to(value[None], (count,) + value.shape), axes, 0, 0)


def swapped(value, axis):
    return lax.ppermute(value, axis, [(0, 1), (1, 0)])


def rows_of_all_y(weight, core):
    rows, features = weight.shape
    half = lax.dynamic_slice_in_dim(weight, core * (rows // 2), rows // 2, 0)
    half = half.reshape(rows // 2, NY, NZ, 128).transpose(0, 2, 1, 3).reshape(rows // 2, features)
    mine = spread(half, "y", NY).reshape(NY * rows // 2, features)
    return mine, swapped(mine, "c")


def own_first(value, core):
    return [
        lax.dynamic_index_in_dim(value, i, 1, keepdims=False).reshape(-1, value.shape[-1])
        for i in (core, 1 - core)
    ]


def forward_step(
    core_ref,
    context_ref,
    policy_mine_ref,
    policy_other_ref,
    frozen_mine_ref,
    frozen_other_ref,
    policy_stream_ref,
    frozen_stream_ref,
    targets_ref,
    gains_ref,
    valid_ref,
    hidden_ref,
    stats_ref,
    own_columns_ref,
    other_columns_ref,
    frozen_ref,
):
    step = pl.program_id(0)
    tokens = hidden_ref.shape[2]

    @pl.when(step == 0)
    def _():
        hidden_ref[...] = policy_stream_ref[...].astype(jnp.float32)
        frozen_ref[...] = frozen_stream_ref[...].astype(jnp.float32)

    policy_context = context_ref[:tokens, :]
    frozen_context = context_ref[tokens:, :]
    for sums, half, weight, context in (
        (hidden_ref, 0, policy_mine_ref, policy_context),
        (hidden_ref, 1, policy_other_ref, policy_context),
        (frozen_ref, 0, frozen_mine_ref, frozen_context),
        (frozen_ref, 1, frozen_other_ref, frozen_context),
    ):
        sums[half] += lax.dot_general(
            weight[...], context, (((1,), (1,)), ((), ())), preferred_element_type=jnp.float32
        )

    def move(columns_ref):
        for i in range(2 * NY):
            e, y = i // NY, i % NY
            columns_ref[y // 2, 2 * (y % 2) + lax.div(step, 2), :, e * 128 : (e + 1) * 128] = (
                context_ref[:tokens, i * 128 : (i + 1) * 128]
            )

    @pl.when(lax.rem(step, 2) == core_ref[0])
    def _():
        move(own_columns_ref)

    @pl.when(lax.rem(step, 2) != core_ref[0])
    def _():
        move(other_columns_ref)

    @pl.when(step == NZ // 2 - 1)
    def _():
        totals = [0.0] * 4
        for half in range(2):
            target = targets_ref[half].astype(jnp.float32)
            for model, hidden in enumerate((hidden_ref[half], frozen_ref[half])):
                gain = gains_ref[:, 2 * model + half : 2 * model + half + 1]
                terms = (hidden * hidden, hidden * (gain * target))
                for i, term in enumerate(terms):
                    totals[2 * model + i] += jnp.sum(term, axis=0, keepdims=True)
        totals[1], totals[3] = totals[1] * valid_ref[...], totals[3] * valid_ref[...]
        for i in range(4):
            stats_ref[:, i : i + 1, :] = jnp.broadcast_to(
                totals[i][None], (2 * NZ, 1, tokens)
            )


def forward(core, contexts, policy_rows, frozen_rows, streams, gains, valid):
    half_rows, features = policy_rows[0].shape
    tokens = contexts.shape[0] // 2
    depth = features // (NZ // 2)

    def whole(*shape):
        return pl.BlockSpec(shape, lambda z: (0,) * len(shape))

    weight = pl.BlockSpec((half_rows, depth), lambda z: (0, z))
    block = (2, half_rows, tokens)
    columns = (2, NX, tokens, 256)
    return pl.pallas_call(
        forward_step,
        grid=(NZ // 2,),
        in_specs=[
            pl.BlockSpec(memory_space=pltpu.SMEM),
            pl.BlockSpec((2 * tokens, depth), lambda z: (0, z)),
            weight,
            weight,
            weight,
            weight,
            whole(*block),
            whole(*block),
            whole(*block),
            whole(half_rows, 4),
            whole(1, tokens),
        ],
        out_specs=[whole(*block), whole(2 * NZ, 4, tokens), whole(*columns), whole(*columns)],
        out_shape=[
            jax.ShapeDtypeStruct(block, jnp.float32),
            jax.ShapeDtypeStruct((2 * NZ, 4, tokens), jnp.float32),
            jax.ShapeDtypeStruct(columns, jnp.bfloat16),
            jax.ShapeDtypeStruct(columns, jnp.bfloat16),
        ],
        scratch_shapes=[pltpu.VMEM(block, jnp.float32)],
        compiler_params=pltpu.CompilerParams(vmem_limit_bytes=56 * 2**20),
        cost_estimate=pl.CostEstimate(
            flops=8 * half_rows * tokens * features,
            bytes_accessed=2 * features * (4 * half_rows + 3 * tokens),
            transcendentals=0,
        ),
    )(core[None], contexts, *policy_rows, *frozen_rows, *streams, gains, valid)


def shards(
    policy_context,
    frozen_context,
    policy_stream,
    frozen_stream,
    targets,
    policy_gain,
    frozen_gain,
    policy_weight,
    frozen_weight,
    valid_lengths,
    pair_rows,
):
    rows, tokens_here = policy_stream.shape
    seq_len = tokens_here // valid_lengths.shape[0]
    seqs = valid_lengths.shape[0] // NY
    tokens = tokens_here // NY
    z_hi, x, core, y = (lax.axis_index(name) for name in ("zh", "x", "c", "y"))

    contexts = jnp.stack(
        [policy_context.reshape(NY, tokens, 128), frozen_context.reshape(NY, tokens, 128)], axis=1
    )
    contexts = lax.all_to_all(contexts, "y", 0, 0)
    contexts = contexts.transpose(1, 2, 0, 3).reshape(2 * tokens, NY * 128)
    contexts = lax.all_gather(contexts, "zl", axis=1, tiled=True)

    frozen_rows = rows_of_all_y(frozen_weight, core)
    policy_rows = rows_of_all_y(policy_weight, core)
    streams = jnp.stack(
        [
            s.reshape(rows, NY, tokens).transpose(1, 0, 2)
            for s in (policy_stream, frozen_stream, targets)
        ],
        axis=1,
    )
    streams = lax.all_to_all(streams, "y", 0, 0)
    streams = streams.reshape(NY, 3, 2, rows // 2, tokens)
    streams = [jnp.stack(own_first(streams[:, i], core)) for i in range(3)]
    gains = spread(jnp.stack([policy_gain, frozen_gain]), "y", NY)
    gains = gains.reshape(NY, 2, 2, rows // 2, 1)
    gains = jnp.concatenate([g for i in range(2) for g in own_first(gains[:, i], core)], axis=1)
    other_targets = swapped(streams[2], "c")
    lengths = lax.dynamic_slice_in_dim(valid_lengths, y * seqs, seqs, 0)
    positions = lax.broadcasted_iota(jnp.int32, (seqs, seq_len), 1)
    valid = (positions < lengths[:, None]).astype(jnp.float32).reshape(1, tokens)
    contexts, frozen_rows, policy_rows, streams, gains, other_targets, valid = (
        lax.optimization_barrier(
            (contexts, frozen_rows, policy_rows, streams, gains, other_targets, valid)
        )
    )
    policy_hidden, stats, columns, other_columns = forward(
        core, contexts, policy_rows, frozen_rows, streams, gains, valid
    )
    stats = lax.all_to_all(stats, ("zh", "zl"), 0, 0).reshape(2, NZ, 4, tokens)
    stats = jnp.sum(stats, axis=1)
    other_hidden = swapped(policy_hidden, "c")
    other_columns = swapped(other_columns, "c")

    scales = lax.rsqrt(stats[:, 0::2] / D + epsilon)
    gap_of_token = scales[:, 0] * stats[:, 1] - scales[:, 1] * stats[:, 3]
    own_gaps = jnp.sum(gap_of_token.reshape(2 * seqs, seq_len), axis=1)
    scalars = jnp.stack([scales[:, 0], stats[:, 1]], axis=1)
    scalars = lax.dynamic_index_in_dim(scalars, z_hi, 0, keepdims=False)
    scalars = jnp.concatenate([scalars, valid])
    told = jnp.concatenate([own_gaps, scalars.reshape(-1)])
    told = spread(told, ("x", "c", "y"), NX * 2 * NY)
    told, other_columns, other_hidden = lax.optimization_barrier(
        (told, other_columns, other_hidden)
    )
    gaps = told[:, : 2 * seqs].reshape(NX, 2, NY, 2, seqs).transpose(3, 0, 1, 2, 4).reshape(-1)
    other_scalars = lax.dynamic_index_in_dim(told, (x * 2 + 1 - core) * NY + y, 0, keepdims=False)
    other_scalars = other_scalars[2 * seqs :].reshape(3, tokens)

    total_seqs = gaps.shape[0]
    pair_count = pair_rows.shape[0]
    row_ids = lax.broadcasted_iota(jnp.int32, (pair_count, total_seqs), 1)
    signs = (row_ids == pair_rows[:, 0:1]).astype(jnp.float32) - (
        row_ids == pair_rows[:, 1:2]
    ).astype(jnp.float32)
    margins = beta_scale * jnp.sum(signs * gaps[None, :], axis=1)
    loss = jnp.sum(jax.nn.softplus(-margins))
    slopes = -jax.nn.sigmoid(-margins)

    policy_gain = gains[:, :2].T[:, :, None]

    def hidden_grad_of(core_of_tokens, scale, dotted, valid, gain, all_targets, all_hidden):
        own_ids = (
            ((lax.axis_index(("zh", "x")) * 2 + core_of_tokens) * NY + y) * seqs
            + lax.broadcasted_iota(jnp.int32, (1, seqs), 1)
        )
        own_chosen = (pair_rows[:, 0:1] == own_ids).astype(jnp.float32)
        own_rejected = (pair_rows[:, 1:2] == own_ids).astype(jnp.float32)
        coef = beta_scale * jnp.sum(slopes[:, None] * (own_chosen - own_rejected), axis=0)
        step_size = jnp.broadcast_to(coef[:, None], (seqs, seq_len)).reshape(tokens) * valid * scale
        correction = dotted * scale * scale / D
        grad = step_size * (gain * all_targets.astype(jnp.float32) - all_hidden * correction)
        grad = grad.astype(jnp.bfloat16)
        grad = jnp.where(core_of_tokens == 0, grad, grad[::-1]).reshape(2, NY, rows // 2, tokens)
        return grad.transpose(1, 0, 2, 3).reshape(NY * rows, tokens)

    own_grad = hidden_grad_of(core, *scalars, policy_gain, streams[2], policy_hidden)
    other_grad = hidden_grad_of(
        1 - core, *other_scalars, policy_gain[::-1], other_targets, other_hidden
    )
    hidden_grad = jnp.concatenate([own_grad, other_grad], axis=1)
    columns = jnp.concatenate([columns, other_columns], axis=2)

    def grad_of(z_hi):
        piece = lax.dynamic_index_in_dim(columns, z_hi, 0, keepdims=False)
        return jnp.stack(
            [jnp.dot(hidden_grad, piece[i], preferred_element_type=jnp.float32) for i in range(NX)]
        )

    z_order = (1 - z_hi, z_hi)
    sums = []
    for z in z_order:
        grad = grad_of(z).astype(jnp.bfloat16).reshape(NX * NY, rows, 256)
        grad = lax.all_to_all(grad, ("x", "y"), 0, 0)
        sums.append(jnp.sum(grad.astype(jnp.float32), axis=0))
    weight_grad = sums[1] + swapped(sums[0].astype(jnp.bfloat16), "zh").astype(jnp.float32)
    return (weight_grad, margins, loss)


def solution(mesh):
    dp, blk = ("zh", "x", "c"), ("y", "zl")
    fine = Mesh(mesh.devices.reshape(2, NX, 2, NY, NZ), dp + blk)
    placed = (
        P(dp, blk),
        P(dp, blk),
        P(blk, dp),
        P(blk, dp),
        P(blk, dp),
        P(blk),
        P(blk),
        P(blk, None),
        P(blk, None),
        P(dp),
        P(),
    )
    return jax.shard_map(
        shards, mesh=fine, in_specs=placed, out_specs=(P(blk, dp), P(), P()), check_vma=False
    )
```
